32 devices in a mesh: tm: 8 (over z, x), obs: 4 (over y, core).
Axes of the slice: x: 2, y: 2, z: 4, core: 2. Of those that a mesh axis runs over, the one named last changes fastest.
Arguments:
- observed: float32 [32, 2048], P('tm', 'obs'), may hold values from -6 to 6
- slot_site: int32 [32, 2048], P('tm', 'obs'), may hold values from 0 to 16383
- live_count: int32 [32, 4], P('tm', 'obs'), may hold values from 128 to 512
- site_feature: float32 [16384, 128], replicated, may hold values from -0.5 to 0.5
- site_precision: float32 [16384], replicated, may hold values from 0.5 to 8
- time_scale: float32 [128], replicated, may hold values from 4 to 200
- variance: float32 [128], replicated, may hold values from 0.5 to 2
Outputs:
- filtered_mean: float32 [32, 128], P('tm')
The draws below stay inside these ranges and needn't reach their ends.
Inputs may be any that keep to these rules, and one draw needn't show every extreme that they name: `slot_site`: slot sites index the sensor locations. `live_count`: live slots of a group come first.
All inputs are finite; a program needn't handle non-finite values.
Results may differ from the reference program's by a relative error of at most 0.0003.
Values sent between devices are 32-bit elements; how exact they have to be, the bound alone decides.
A program may use at most 192 MiB of HBM per device.

```python
import math
import jax
import jax.numpy as jnp
from jax import lax

BASIS = 128
STEPS = 32
OBS_DEV = 512
GROUPS = 4
SLOTS = 2048
SITES = 16384


def with_ends(drawn, key, low, top_value):
    extent = drawn.shape
    place = [jax.random.randint(jax.random.fold_in(key, axis), (), 0, extent[axis]) for axis in range(len(extent))]
    drawn = drawn.at[tuple(place)].set(low)
    longest = extent.index(max(extent))
    place[longest] = (place[longest] + 1) % extent[longest]
    return drawn.at[tuple(place)].set(top_value)


def levels(rng, shape, pieces, least, high):
    loudness = 1.0
    for dim, shards_of in pieces:
        heights = jax.random.uniform(jax.random.fold_in(jax.random.fold_in(rng, 6), dim), (shards_of,), jnp.float32, least / len(pieces), high / len(pieces))
        loudness = loudness * jnp.repeat(jnp.exp(heights), shape[dim] // shards_of).reshape((-1,) + (1,) * (len(shape) - 1 - dim))
    return loudness


def centred(key, shape, width, limit, pieces=(), kind=jnp.bfloat16):
    drawn = width * jax.random.normal(key, shape, jnp.float32)
    if pieces:
        drawn = drawn * levels(key, shape, pieces, -0.22, 0.18)
    return jnp.clip(drawn, -limit, limit).astype(kind)


def setup_inputs(seed: int = 0) -> dict:
    key_of = jax.random.split(jax.random.key(seed), 8)
    observed = centred(key_of[0], (STEPS, SLOTS), 1.0, 6.0, ((0, 8), (1, 4)), jnp.float32)
    slot_site = with_ends(jax.random.randint(key_of[1], (STEPS, SLOTS), 0, SITES), jax.random.fold_in(key_of[1], 1), 0, SITES - 1).astype(jnp.int32)
    live_count = with_ends(jax.random.randint(key_of[2], (STEPS, GROUPS), OBS_DEV // 4, OBS_DEV + 1), jax.random.fold_in(key_of[2], 1), OBS_DEV // 4, OBS_DEV).astype(jnp.int32)
    site_feature = centred(key_of[3], (SITES, BASIS), BASIS ** -0.5, 0.5, (), jnp.float32)
    site_precision = jnp.clip(jnp.exp(jax.random.uniform(key_of[4], (SITES,), jnp.float32, math.log(0.5), math.log(8.0))), 0.5, 8.0)
    time_scale = jnp.clip(jnp.exp(jax.random.uniform(key_of[5], (BASIS,), jnp.float32, math.log(4.0), math.log(200.0))), 4.0, 200.0)
    variance = jnp.clip(jnp.exp(jax.random.uniform(key_of[6], (BASIS,), jnp.float32, math.log(0.5), math.log(2.0))), 0.5, 2.0)
    return dict(observed=observed, slot_site=slot_site, live_count=live_count, site_feature=site_feature, site_precision=site_precision, time_scale=time_scale, variance=variance)


def matmul_high(left, right):
    return jnp.dot(left.astype(jnp.float32), right.astype(jnp.float32), precision=lax.Precision.HIGHEST, preferred_element_type=jnp.float32)

def gain_inverse(covariance, precision_mat):
    identity = jnp.eye(covariance.shape[0], dtype=covariance.dtype)
    factor_low = lax.linalg.cholesky(covariance)
    right_side = matmul_high(factor_low.T, precision_mat)
    inner_mat = identity + matmul_high(right_side, factor_low)
    inner_low = lax.linalg.cholesky(inner_mat)
    partial_solve = lax.linalg.triangular_solve(inner_low, right_side, left_side=True, lower=True)
    solved = lax.linalg.triangular_solve(inner_low, partial_solve, left_side=True, lower=True, transpose_a=True)
    return identity - matmul_high(factor_low, solved)

def combine_full(earlier, later):
    trans_e, mean_e, cov_e, eta_e, prec_e = earlier
    trans_l, mean_l, cov_l, eta_l, prec_l = later
    gain = gain_inverse(cov_e, prec_l)
    moved = matmul_high(trans_l, gain)
    trans_new = matmul_high(moved, trans_e)
    mean_new = matmul_high(moved, mean_e + matmul_high(cov_e, eta_l)) + mean_l
    cov_new = matmul_high(matmul_high(moved, cov_e), trans_l.T) + cov_l
    backward = matmul_high(trans_e.T, gain.T)
    eta_new = matmul_high(backward, eta_l - matmul_high(prec_l, mean_e)) + eta_e
    prec_new = matmul_high(matmul_high(backward, prec_l), trans_e) + prec_e
    return (trans_new, mean_new, cov_new, eta_new, prec_new)

def combine_reduce(prior_mean, prior_cov, later):
    trans_l, mean_l, cov_l, eta_l, prec_l = later
    gain = gain_inverse(prior_cov, prec_l)
    moved = matmul_high(trans_l, gain)
    mean_new = matmul_high(moved, prior_mean + matmul_high(prior_cov, eta_l)) + mean_l
    cov_new = matmul_high(matmul_high(moved, prior_cov), trans_l.T) + cov_l
    return (mean_new, cov_new)

def matern_blocks(time_scale, variance):
    rate = jnp.sqrt(jnp.float32(3.0)) / time_scale
    decay = jnp.exp(-rate)
    twice = 2.0 * rate
    decay_two = jnp.exp(-twice)
    term_now = twice ** 3 / 6.0
    series = term_now
    for degree in range(4, 17):
        term_now = term_now * twice / degree
        series = series + term_now
    noise_pp = variance * decay_two * series
    noise_pv = 2.0 * rate ** 3 * decay_two * variance
    noise_vv = rate ** 2 * variance * decay_two * (jnp.expm1(twice) + twice - 0.5 * twice ** 2)
    trans = jnp.block([[jnp.diag(decay * (1.0 + rate)), jnp.diag(decay)], [jnp.diag(-rate ** 2 * decay), jnp.diag(decay * (1.0 - rate))]])
    noise = jnp.block([[jnp.diag(noise_pp), jnp.diag(noise_pv)], [jnp.diag(noise_pv), jnp.diag(noise_vv)]])
    station = jnp.diag(jnp.concatenate([variance, rate ** 2 * variance]))
    return (trans, noise, station)

def step_element(trans_pred, cov_pred, gram_block, info_vec):
    basis_n = gram_block.shape[0]
    states_n = 2 * basis_n
    identity = jnp.eye(states_n, dtype=cov_pred.dtype)
    zero_vec = jnp.zeros((states_n,), cov_pred.dtype)
    zero_mat = jnp.zeros((states_n, states_n), cov_pred.dtype)
    prec_full = jnp.pad(gram_block, ((0, basis_n), (0, basis_n)))
    info_full = jnp.pad(info_vec, ((0, basis_n),))
    predicted = (trans_pred, zero_vec, cov_pred, zero_vec, zero_mat)
    updated = (identity, zero_vec, zero_mat, info_full, prec_full)
    return combine_full(predicted, updated)

def reference(observed, slot_site, live_count, site_feature, site_precision, time_scale, variance):
    slot_index = jnp.arange(SLOTS, dtype=jnp.int32)
    group_of = slot_index // OBS_DEV
    rank_of = slot_index % OBS_DEV
    live = (rank_of[None, :] < live_count[:, group_of]).astype(jnp.float32)
    weight = site_precision[slot_site] * live
    feature = site_feature[slot_site]
    weighted = feature * weight[:, :, None]
    gram = jnp.einsum('tna,tnb->tab', weighted, feature, precision=lax.Precision.HIGHEST)
    info = jnp.einsum('tn,tna->ta', observed, weighted, precision=lax.Precision.HIGHEST)
    trans, noise, station = matern_blocks(time_scale, variance)
    first = step_element(jnp.zeros_like(trans), station, gram[0], info[0])

    def advance(carry, inputs):
        prior_mean, prior_cov = carry
        gram_step, info_step = inputs
        element = step_element(trans, noise, gram_step, info_step)
        mean_new, cov_new = combine_reduce(prior_mean, prior_cov, element)
        return ((mean_new, cov_new), mean_new)
    carry_out, means = lax.scan(advance, (first[1], first[2]), (gram[1:], info[1:]))
    all_means = jnp.concatenate([first[1][None, :], means], axis=0)
    return all_means[:, :BASIS]
```

```python
import functools

import jax
import jax.numpy as jnp
from jax import lax
from jax.experimental import pallas as pl
from jax.experimental.pallas import tpu as pltpu
from jax.sharding import PartitionSpec as P

F32 = jnp.float32
BF16 = jnp.bfloat16


def dot_full(left, right):
    return jnp.dot(left, right, precision=lax.Precision.HIGHEST, preferred_element_type=F32)


def split(value):
    high = value.astype(BF16)
    return high, (value - high.astype(F32)).astype(BF16)


def dot_three(left, right):
    left_high, left_low = split(left)
    right_high, right_low = split(right)
    sides = jnp.concatenate([left_high, left_low], axis=1)
    tops = jnp.concatenate([right_high, right_high], axis=0)
    first = jnp.dot(sides, tops, preferred_element_type=F32)
    return first + jnp.dot(left_high, right_low, preferred_element_type=F32)


def matern_rows(time_scale, variance):
    rate = jnp.sqrt(F32(3.0)) / time_scale
    decay = jnp.exp(-rate)
    twice = 2.0 * rate
    decay_two = jnp.exp(-twice)
    term_now = twice**3 / 6.0
    series = term_now
    for degree in range(4, 17):
        term_now = term_now * twice / degree
        series = series + term_now
    noise_pp = variance * decay_two * series
    noise_pv = 2.0 * rate**3 * decay_two * variance
    noise_vv = rate**2 * variance * decay_two * (jnp.expm1(twice) + twice - 0.5 * twice**2)
    rows = [
        decay * (1.0 + rate),
        decay,
        -(rate**2) * decay,
        decay * (1.0 - rate),
        noise_pp,
        noise_pv,
        noise_vv,
        variance,
        rate**2 * variance,
    ]
    rows += [jnp.zeros_like(rate)] * (16 - len(rows))
    return jnp.stack(rows)


def filter_kernel(rows_ref, gram_ref, info_ref, mean_ref, coef_ref):
    steps, basis, _ = gram_ref.shape
    row_i = lax.broadcasted_iota(jnp.int32, (basis, basis), 0)
    col_i = lax.broadcasted_iota(jnp.int32, (basis, basis), 1)
    eye = (row_i == col_i).astype(F32)

    def wide(index):
        return jnp.broadcast_to(rows_ref[index : index + 1, :], (basis, basis))

    right = [wide(index) for index in range(4)]
    left = [value.T for value in right]
    pairs = [(0, 0), (0, 1), (1, 1), (0, 2), (1, 2), (0, 3), (1, 3), (2, 2), (2, 3), (3, 3)]
    for place, (one, two) in enumerate(pairs):
        scale = 0.5 if one == two else 1.0
        coef_ref[place] = scale * left[one] * right[two]
    coef_ref[10] = 0.5 * wide(4) * eye
    coef_ref[11] = wide(5) * eye
    coef_ref[12] = 0.5 * wide(6) * eye
    step_a = rows_ref[0:1, :]
    step_b = rows_ref[1:2, :]
    step_c = rows_ref[2:3, :]
    step_d = rows_ref[3:4, :]

    def advance(step, carry):
        cov_pp, cov_pv, cov_vv, mean_p, mean_v = carry
        gram = gram_ref[step]
        info = info_ref[step]
        both = jnp.concatenate([cov_pp, cov_pv], axis=1)
        seen = dot_full(gram, both)
        target = eye + seen[:, :basis].T
        bound = jnp.max(jnp.sum(jnp.abs(target), axis=1))
        scale = 2.0 / (1.0 + bound)
        start = jnp.concatenate([eye - scale * target, scale * eye], axis=0)

        def squaring(state):
            radius, pair = state
            product = dot_three(pair, pair[:basis])
            pair = jnp.concatenate([product[:basis], pair[basis:] + product[basis:]], axis=0)
            return radius * radius, pair

        _, pair = lax.while_loop(lambda s: s[0] > 3e-3, squaring, ((bound - 1.0) * 0.5 * scale, start))

        def polish(state):
            count, _, inverse = state
            rest = eye - dot_full(target, inverse)
            size = jnp.max(jnp.abs(rest))
            return count + 1, size, inverse + dot_full(inverse, rest)

        _, _, gain = lax.while_loop(
            lambda s: jnp.logical_and(s[0] < 12, s[1] > 2e-3),
            polish,
            (jnp.int32(0), F32(1.0), pair[basis:]),
        )
        both = dot_full(gain, both)
        new_pp = both[:, :basis]
        new_pv = both[:, basis:]
        new_vv = cov_vv - dot_full(seen[:, basis:].T, new_pv)
        residual = info - dot_full(mean_p, gram)
        moved = dot_full(residual, both)
        mean_p = mean_p + moved[:, :basis]
        mean_v = mean_v + moved[:, basis:]
        mean_ref[step] = mean_p
        new_vp = new_pv.T
        half_pp = coef_ref[0] * new_pp + coef_ref[1] * new_pv + coef_ref[2] * new_vv + coef_ref[10]
        half_vv = coef_ref[7] * new_pp + coef_ref[8] * new_pv + coef_ref[9] * new_vv + coef_ref[12]
        next_pv = (
            coef_ref[3] * new_pp
            + coef_ref[4] * new_vp
            + coef_ref[5] * new_pv
            + coef_ref[6] * new_vv
            + coef_ref[11]
        )
        return (
            half_pp + half_pp.T,
            next_pv,
            half_vv + half_vv.T,
            step_a * mean_p + step_b * mean_v,
            step_c * mean_p + step_d * mean_v,
        )

    zero_row = jnp.zeros((8, basis), F32)
    first = (wide(7) * eye, jnp.zeros((basis, basis), F32), wide(8) * eye, zero_row, zero_row)
    lax.fori_loop(0, steps, advance, first)


def run_filter(rows, gram, info):
    steps, basis, _ = gram.shape
    return pl.pallas_call(
        filter_kernel,
        out_shape=jax.ShapeDtypeStruct((steps, 8, basis), F32),
        in_specs=[pl.BlockSpec(memory_space=pltpu.VMEM)] * 3,
        out_specs=pl.BlockSpec(memory_space=pltpu.VMEM),
        scratch_shapes=[pltpu.VMEM((13, basis, basis), F32)],
        compiler_params=pltpu.CompilerParams(vmem_limit_bytes=32 * 1024 * 1024),
    )(rows, gram, info)


def body(observed, slot_site, live_count, site_feature, site_precision, time_scale, variance):
    steps_local, slots_local = observed.shape
    basis = site_feature.shape[1]
    rank_of = jnp.arange(slots_local, dtype=jnp.int32)
    live = (rank_of[None, :] < live_count).astype(F32)
    weight = site_precision[slot_site] * live
    feature = site_feature[slot_site]
    weighted = feature * weight[:, :, None]
    sides = jnp.concatenate([feature, jnp.broadcast_to(observed[:, :, None], (steps_local, slots_local, 8))], axis=2)
    part = jnp.einsum("tna,tnb->tab", sides, weighted, precision=lax.Precision.HIGHEST)
    summed = lax.psum(part, "obs")
    every = lax.all_gather(summed, "tm", axis=0, tiled=True)
    means = run_filter(matern_rows(time_scale, variance), every[:, :basis], every[:, basis:])
    block = lax.axis_index("tm")
    return lax.dynamic_slice(means[:, 0, :], (block * steps_local, 0), (steps_local, basis))


def solution(mesh):
    in_specs = (P("tm", "obs"), P("tm", "obs"), P("tm", "obs"), P(), P(), P(), P())
    out_specs = P("tm", None)
    return jax.shard_map(body, mesh=mesh, in_specs=in_specs, out_specs=out_specs, check_vma=False)
```

```python
import functools

import jax
import jax.numpy as jnp
from jax import lax
from jax.experimental import pallas as pl
from jax.experimental.pallas import tpu as pltpu
from jax.sharding import PartitionSpec as P

F32 = jnp.float32
BF16 = jnp.bfloat16
MESH = pl.DeviceIdType.MESH


def dot_full(left, right):
    return jnp.dot(left, right, precision=lax.Precision.HIGHEST, preferred_element_type=F32)


def split(value):
    high = value.astype(BF16)
    return high, (value - high.astype(F32)).astype(BF16)


def dot_three(left, right):
    left_high, left_low = split(left)
    right_high, right_low = split(right)
    sides = jnp.concatenate([left_high, left_low], axis=1)
    tops = jnp.concatenate([right_high, right_high], axis=0)
    first = jnp.dot(sides, tops, preferred_element_type=F32)
    return first + jnp.dot(left_high, right_low, preferred_element_type=F32)


def matern_rows(time_scale, variance):
    rate = jnp.sqrt(F32(3.0)) / time_scale
    decay = jnp.exp(-rate)
    twice = 2.0 * rate
    decay_two = jnp.exp(-twice)
    term_now = twice**3 / 6.0
    series = term_now
    for degree in range(4, 17):
        term_now = term_now * twice / degree
        series = series + term_now
    noise_pp = variance * decay_two * series
    noise_pv = 2.0 * rate**3 * decay_two * variance
    noise_vv = rate**2 * variance * decay_two * (jnp.expm1(twice) + twice - 0.5 * twice**2)
    rows = [
        decay * (1.0 + rate),
        decay,
        -(rate**2) * decay,
        decay * (1.0 - rate),
        noise_pp,
        noise_pv,
        noise_vv,
        variance,
        rate**2 * variance,
    ]
    rows += [jnp.zeros_like(rate)] * (16 - len(rows))
    return jnp.stack(rows)


def filter_kernel(rows_ref, every_ref, mean_ref, coef_ref):
    steps, _, basis = every_ref.shape
    row_i = lax.broadcasted_iota(jnp.int32, (basis, basis), 0)
    col_i = lax.broadcasted_iota(jnp.int32, (basis, basis), 1)
    eye = (row_i == col_i).astype(F32)

    def wide(index):
        return jnp.broadcast_to(rows_ref[index : index + 1, :], (basis, basis))

    right = [wide(index) for index in range(4)]
    left = [value.T for value in right]
    pairs = [(0, 0), (0, 1), (1, 1), (0, 2), (1, 2), (0, 3), (1, 3), (2, 2), (2, 3), (3, 3)]
    for place, (one, two) in enumerate(pairs):
        scale = 0.5 if one == two else 1.0
        coef_ref[place] = scale * left[one] * right[two]
    coef_ref[10] = 0.5 * wide(4) * eye
    coef_ref[11] = wide(5) * eye
    coef_ref[12] = 0.5 * wide(6) * eye
    step_a = rows_ref[0:1, :]
    step_b = rows_ref[1:2, :]
    step_c = rows_ref[2:3, :]
    step_d = rows_ref[3:4, :]

    def advance(step, carry):
        cov_pp, cov_pv, cov_vv, mean_p, mean_v = carry
        gram = every_ref[step, :basis, :]
        info = every_ref[step, basis : basis + 8, :]
        both = jnp.concatenate([cov_pp, cov_pv], axis=1)
        seen = dot_three(gram, both)
        target = eye + seen[:, :basis].T
        bound = jnp.max(jnp.sum(jnp.abs(target), axis=1))
        scale = 2.0 / (1.0 + bound)
        start = jnp.concatenate([eye - scale * target, scale * eye], axis=0)

        def squaring(state):
            radius, pair = state
            product = dot_three(pair, pair[:basis])
            pair = jnp.concatenate([product[:basis], pair[basis:] + product[basis:]], axis=0)
            return radius * radius, pair

        _, pair = lax.while_loop(lambda s: s[0] > 3e-3, squaring, ((bound - 1.0) * 0.5 * scale, start))

        def polish(state):
            count, _, inverse = state
            rest = eye - dot_three(target, inverse)
            size = jnp.max(jnp.abs(rest))
            return count + 1, size, inverse + dot_three(inverse, rest)

        _, _, gain = lax.while_loop(
            lambda s: jnp.logical_and(s[0] < 12, s[1] > 2e-3),
            polish,
            (jnp.int32(0), F32(1.0), pair[basis:]),
        )
        both = dot_three(gain, both)
        new_pp = both[:, :basis]
        new_pv = both[:, basis:]
        new_vv = cov_vv - dot_three(seen[:, basis:].T, new_pv)
        residual = info - dot_full(mean_p, gram)
        moved = dot_full(residual, both)
        mean_p = mean_p + moved[:, :basis]
        mean_v = mean_v + moved[:, basis:]
        mean_ref[step] = mean_p
        new_vp = new_pv.T
        half_pp = coef_ref[0] * new_pp + coef_ref[1] * new_pv + coef_ref[2] * new_vv + coef_ref[10]
        half_vv = coef_ref[7] * new_pp + coef_ref[8] * new_pv + coef_ref[9] * new_vv + coef_ref[12]
        next_pv = (
            coef_ref[3] * new_pp
            + coef_ref[4] * new_vp
            + coef_ref[5] * new_pv
            + coef_ref[6] * new_vv
            + coef_ref[11]
        )
        return (
            half_pp + half_pp.T,
            next_pv,
            half_vv + half_vv.T,
            step_a * mean_p + step_b * mean_v,
            step_c * mean_p + step_d * mean_v,
        )

    zero_row = jnp.zeros((8, basis), F32)
    first = (wide(7) * eye, jnp.zeros((basis, basis), F32), wide(8) * eye, zero_row, zero_row)
    lax.fori_loop(0, steps, advance, first)


def gather_kernel(part_ref, all_ref, recv_ref, rs_send, rs_recv, tm_send, tm_recv, ob_send, ob_recv):
    blocks, groups, chunk, _ = all_ref.shape
    block = lax.axis_index("tm")
    group = lax.axis_index("obs")

    def to_block(distance):
        return {"tm": lax.rem(block + distance, blocks)}

    def to_group(distance):
        return {"obs": lax.rem(group + distance, groups)}

    barrier = pltpu.get_barrier_semaphore()
    for distance in range(1, groups):
        pl.semaphore_signal(barrier, inc=1, device_id=to_group(distance), device_id_type=MESH)

    def greet(distance, carry):
        pl.semaphore_signal(barrier, inc=1, device_id=to_block(distance), device_id_type=MESH)
        return carry

    lax.fori_loop(1, blocks, greet, 0)
    pl.semaphore_wait(barrier, groups + blocks - 2)

    def scatter(distance):
        peer = lax.rem(group + distance, groups)
        return pltpu.make_async_remote_copy(
            src_ref=part_ref.at[peer],
            dst_ref=recv_ref.at[distance - 1],
            send_sem=rs_send.at[distance - 1],
            recv_sem=rs_recv.at[distance - 1],
            device_id=to_group(distance),
            device_id_type=MESH,
        )

    for distance in range(1, groups):
        scatter(distance).start()
    total = part_ref[group]
    for distance in range(1, groups):
        scatter(distance).wait_recv()
        total = total + recv_ref[distance - 1]
    all_ref[block, group] = total

    def along(distance, source):
        return pltpu.make_async_remote_copy(
            src_ref=all_ref.at[source, group],
            dst_ref=all_ref.at[source, group],
            send_sem=tm_send.at[distance],
            recv_sem=tm_recv.at[distance],
            device_id=to_block(distance),
            device_id_type=MESH,
        )

    def across(distance, source, step, owner):
        return pltpu.make_async_remote_copy(
            src_ref=all_ref.at[source, owner],
            dst_ref=all_ref.at[source, owner],
            send_sem=ob_send.at[distance, step - 1],
            recv_sem=ob_recv.at[distance, step - 1],
            device_id=to_group(step),
            device_id_type=MESH,
        )

    def send_along(distance, carry):
        along(distance, block).start()
        return carry

    lax.fori_loop(1, blocks, send_along, 0)
    for step in range(1, groups):
        across(0, block, step, group).start()

    def relay(distance, carry):
        source = lax.rem(block - distance + blocks, blocks)
        along(distance, source).wait_recv()
        for step in range(1, groups):
            across(distance, source, step, group).start()
        return carry

    lax.fori_loop(1, blocks, relay, 0)

    def finish(distance, carry):
        source = lax.rem(block - distance + blocks, blocks)
        for step in range(1, groups):
            owner = lax.rem(group - step + groups, groups)
            across(distance, source, step, owner).wait_recv()
            across(distance, source, step, group).wait_send()
        return carry

    lax.fori_loop(0, blocks, finish, 0)

    def sent(distance, carry):
        along(distance, block).wait_send()
        return carry

    lax.fori_loop(1, blocks, sent, 0)
    for distance in range(1, groups):
        scatter(distance).wait_send()


def run_gather(part, blocks):
    groups, chunk, basis = part.shape
    dma = pltpu.SemaphoreType.DMA
    return pl.pallas_call(
        gather_kernel,
        out_shape=jax.ShapeDtypeStruct((blocks, groups, chunk, basis), F32),
        in_specs=[pl.BlockSpec(memory_space=pltpu.VMEM)],
        out_specs=pl.BlockSpec(memory_space=pltpu.VMEM),
        scratch_shapes=[
            pltpu.VMEM((groups - 1, chunk, basis), F32),
            dma((groups - 1,)),
            dma((groups - 1,)),
            dma((blocks,)),
            dma((blocks,)),
            dma((blocks, groups - 1)),
            dma((blocks, groups - 1)),
        ],
        compiler_params=pltpu.CompilerParams(
            collective_id=0, has_side_effects=True, vmem_limit_bytes=32 * 1024 * 1024
        ),
    )(part)


def run_filter(rows, every):
    steps, _, basis = every.shape
    return pl.pallas_call(
        filter_kernel,
        out_shape=jax.ShapeDtypeStruct((steps, 8, basis), F32),
        in_specs=[pl.BlockSpec(memory_space=pltpu.VMEM)] * 2,
        out_specs=pl.BlockSpec(memory_space=pltpu.VMEM),
        scratch_shapes=[pltpu.VMEM((13, basis, basis), F32)],
        compiler_params=pltpu.CompilerParams(vmem_limit_bytes=32 * 1024 * 1024),
    )(rows, every)


def body(observed, slot_site, live_count, site_feature, site_precision, time_scale, variance):
    steps_local, slots_local = observed.shape
    basis = site_feature.shape[1]
    blocks, groups = lax.axis_size("tm"), lax.axis_size("obs")
    rank_of = jnp.arange(slots_local, dtype=jnp.int32)
    live = (rank_of[None, :] < live_count).astype(F32)
    weight = site_precision[slot_site] * live
    feature = site_feature[slot_site]
    weighted = feature * weight[:, :, None]
    values = jnp.broadcast_to(observed[:, :, None], (steps_local, slots_local, 16))
    sides = jnp.concatenate([feature, values], axis=2)
    part = jnp.einsum("tna,tnb->tab", sides, weighted, precision=lax.Precision.HIGHEST)
    height = basis + 16
    every = run_gather(part.reshape(groups, steps_local * height // groups, basis), blocks)
    every = every.reshape(blocks * steps_local, height, basis)
    means = run_filter(matern_rows(time_scale, variance), every)
    block = lax.axis_index("tm")
    return lax.dynamic_slice(means[:, 0, :], (block * steps_local, 0), (steps_local, basis))


def solution(mesh):
    in_specs = (P("tm", "obs"), P("tm", "obs"), P("tm", "obs"), P(), P(), P(), P())
    out_specs = P("tm", None)
    return jax.shard_map(body, mesh=mesh, in_specs=in_specs, out_specs=out_specs, check_vma=False)
```

```python
import functools

import jax
import jax.numpy as jnp
from jax import lax
from jax.experimental import pallas as pl
from jax.experimental.pallas import tpu as pltpu
from jax.sharding import PartitionSpec as P

F32 = jnp.float32
BF16 = jnp.bfloat16
MESH = pl.DeviceIdType.MESH


def dot_full(left, right):
    return jnp.dot(left, right, precision=lax.Precision.HIGHEST, preferred_element_type=F32)


def split(value):
    high = value.astype(BF16)
    return high, (value - high.astype(F32)).astype(BF16)


def dot_three(left, right):
    left_high, left_low = split(left)
    right_high, right_low = split(right)
    sides = jnp.concatenate([left_high, left_low], axis=1)
    tops = jnp.concatenate([right_high, right_high], axis=0)
    first = jnp.dot(sides, tops, preferred_element_type=F32)
    return first + jnp.dot(left_high, right_low, preferred_element_type=F32)


def matern_rows(time_scale, variance):
    rate = jnp.sqrt(F32(3.0)) / time_scale
    decay = jnp.exp(-rate)
    twice = 2.0 * rate
    decay_two = jnp.exp(-twice)
    term_now = twice**3 / 6.0
    series = term_now
    for degree in range(4, 17):
        term_now = term_now * twice / degree
        series = series + term_now
    noise_pp = variance * decay_two * series
    noise_pv = 2.0 * rate**3 * decay_two * variance
    noise_vv = rate**2 * variance * decay_two * (jnp.expm1(twice) + twice - 0.5 * twice**2)
    rows = [
        decay * (1.0 + rate),
        decay,
        -(rate**2) * decay,
        decay * (1.0 - rate),
        noise_pp,
        noise_pv,
        noise_vv,
        variance,
        rate**2 * variance,
    ]
    rows += [jnp.zeros_like(rate)] * (16 - len(rows))
    return jnp.stack(rows)


def filter_kernel(rows_ref, every_ref, mean_ref, coef_ref):
    steps, _, basis = every_ref.shape
    row_i = lax.broadcasted_iota(jnp.int32, (basis, basis), 0)
    col_i = lax.broadcasted_iota(jnp.int32, (basis, basis), 1)
    eye = (row_i == col_i).astype(F32)

    def wide(index):
        return jnp.broadcast_to(rows_ref[index : index + 1, :], (basis, basis))

    right = [wide(index) for index in range(4)]
    left = [value.T for value in right]
    pairs = [(0, 0), (0, 1), (1, 1), (0, 2), (1, 2), (0, 3), (1, 3), (2, 2), (2, 3), (3, 3)]
    for place, (one, two) in enumerate(pairs):
        scale = 0.5 if one == two else 1.0
        coef_ref[place] = scale * left[one] * right[two]
    coef_ref[10] = 0.5 * wide(4) * eye
    coef_ref[11] = wide(5) * eye
    coef_ref[12] = 0.5 * wide(6) * eye
    step_a = rows_ref[0:1, :]
    step_b = rows_ref[1:2, :]
    step_c = rows_ref[2:3, :]
    step_d = rows_ref[3:4, :]

    def advance(step, carry):
        cov_pp, cov_pv, cov_vv, mean_p, mean_v = carry
        gram = every_ref[step, :basis, :]
        info = every_ref[step, basis : basis + 8, :]
        both = jnp.concatenate([cov_pp, cov_pv], axis=1)
        seen = dot_three(gram, both)
        target = eye + seen[:, :basis].T
        bound = jnp.max(jnp.sum(jnp.abs(target), axis=1))
        scale = 2.0 / (1.0 + bound)
        start = jnp.concatenate([eye - scale * target, scale * eye], axis=0)

        def squaring(state):
            radius, pair = state
            product = dot_three(pair, pair[:basis])
            pair = jnp.concatenate([product[:basis], pair[basis:] + product[basis:]], axis=0)
            return radius * radius, pair

        _, pair = lax.while_loop(lambda s: s[0] > 3e-3, squaring, ((bound - 1.0) * 0.5 * scale, start))

        def polish(state):
            count, _, inverse = state
            rest = eye - dot_three(target, inverse)
            size = jnp.max(jnp.abs(rest))
            return count + 1, size, inverse + dot_three(inverse, rest)

        _, _, gain = lax.while_loop(
            lambda s: jnp.logical_and(s[0] < 12, s[1] > 2e-3),
            polish,
            (jnp.int32(0), F32(1.0), pair[basis:]),
        )
        both = dot_three(gain, both)
        new_pp = both[:, :basis]
        new_pv = both[:, basis:]
        new_vv = cov_vv - dot_three(seen[:, basis:].T, new_pv)
        residual = info - dot_full(mean_p, gram)
        moved = dot_full(residual, both)
        mean_p = mean_p + moved[:, :basis]
        mean_v = mean_v + moved[:, basis:]
        mean_ref[step] = mean_p
        new_vp = new_pv.T
        half_pp = coef_ref[0] * new_pp + coef_ref[1] * new_pv + coef_ref[2] * new_vv + coef_ref[10]
        half_vv = coef_ref[7] * new_pp + coef_ref[8] * new_pv + coef_ref[9] * new_vv + coef_ref[12]
        next_pv = (
            coef_ref[3] * new_pp
            + coef_ref[4] * new_vp
            + coef_ref[5] * new_pv
            + coef_ref[6] * new_vv
            + coef_ref[11]
        )
        return (
            half_pp + half_pp.T,
            next_pv,
            half_vv + half_vv.T,
            step_a * mean_p + step_b * mean_v,
            step_c * mean_p + step_d * mean_v,
        )

    zero_row = jnp.zeros((8, basis), F32)
    first = (wide(7) * eye, jnp.zeros((basis, basis), F32), wide(8) * eye, zero_row, zero_row)
    lax.fori_loop(0, steps, advance, first)


def gather_kernel(part_ref, all_ref, recv_ref, rs_send, rs_recv, tm_send, tm_recv, ob_send, ob_recv, side_send, side_recv):
    blocks, groups, chunk, _ = all_ref.shape
    block = lax.axis_index("tm")
    group = lax.axis_index("obs")

    def to_block(distance):
        return {"tm": lax.rem(block + distance, blocks)}

    def to_group(distance):
        return {"obs": lax.rem(group + distance, groups)}

    barrier = pltpu.get_barrier_semaphore()
    for distance in range(1, groups):
        pl.semaphore_signal(barrier, inc=1, device_id=to_group(distance), device_id_type=MESH)

    def greet(distance, carry):
        pl.semaphore_signal(barrier, inc=1, device_id=to_block(distance), device_id_type=MESH)
        return carry

    lax.fori_loop(1, blocks, greet, 0)
    pl.semaphore_wait(barrier, groups + blocks - 2)

    def scatter(distance):
        peer = lax.rem(group + distance, groups)
        return pltpu.make_async_remote_copy(
            src_ref=part_ref.at[peer],
            dst_ref=recv_ref.at[distance - 1],
            send_sem=rs_send.at[distance - 1],
            recv_sem=rs_recv.at[distance - 1],
            device_id=to_group(distance),
            device_id_type=MESH,
        )

    for distance in range(1, groups):
        scatter(distance).start()
    total = part_ref[group]
    for distance in range(1, groups):
        scatter(distance).wait_recv()
        total = total + recv_ref[distance - 1]
    all_ref[block, group] = total

    def along(distance, source):
        return pltpu.make_async_remote_copy(
            src_ref=all_ref.at[source, group],
            dst_ref=all_ref.at[source, group],
            send_sem=tm_send.at[distance],
            recv_sem=tm_recv.at[distance],
            device_id=to_block(distance),
            device_id_type=MESH,
        )

    pairs = groups // 2
    sibling = group + 1 - 2 * lax.rem(group, 2)

    def owner_of(member, step):
        return lax.rem(member - 2 * step + groups, groups)

    def across(distance, source, step, owner):
        return pltpu.make_async_remote_copy(
            src_ref=all_ref.at[source, owner],
            dst_ref=all_ref.at[source, owner],
            send_sem=ob_send.at[distance, step],
            recv_sem=ob_recv.at[distance, step],
            device_id=to_group(2 * step),
            device_id_type=MESH,
        )

    def aside(distance, source, step, owner):
        return pltpu.make_async_remote_copy(
            src_ref=all_ref.at[source, owner],
            dst_ref=all_ref.at[source, owner],
            send_sem=side_send.at[distance, step],
            recv_sem=side_recv.at[distance, step],
            device_id={"obs": sibling},
            device_id_type=MESH,
        )

    def send_along(distance, carry):
        along(distance, block).start()
        return carry

    def origin(distance):
        return lax.rem(block - distance + blocks, blocks)

    def share(distance):
        source = origin(distance)
        for step in range(1, pairs):
            across(distance, source, step, group).start()
        aside(distance, source, 0, group).start()

    def forward(distance):
        source = origin(distance)
        for step in range(1, pairs):
            owner = owner_of(group, step)
            across(distance, source, step, owner).wait_recv()
            aside(distance, source, step, owner).start()

    lax.fori_loop(1, blocks, send_along, 0)
    share(0)

    def relay(distance, carry):
        along(distance, origin(distance)).wait_recv()
        share(distance)
        forward(distance - 1)
        return carry

    lax.fori_loop(1, blocks, relay, 0)
    forward(blocks - 1)

    def finish(distance, carry):
        source = origin(distance)
        for step in range(pairs):
            aside(distance, source, step, owner_of(sibling, step)).wait_recv()
            aside(distance, source, step, owner_of(group, step)).wait_send()
        for step in range(1, pairs):
            across(distance, source, step, group).wait_send()
        return carry

    lax.fori_loop(0, blocks, finish, 0)

    def sent(distance, carry):
        along(distance, block).wait_send()
        return carry

    lax.fori_loop(1, blocks, sent, 0)
    for distance in range(1, groups):
        scatter(distance).wait_send()


def run_gather(part, blocks):
    groups, chunk, basis = part.shape
    dma = pltpu.SemaphoreType.DMA
    return pl.pallas_call(
        gather_kernel,
        out_shape=jax.ShapeDtypeStruct((blocks, groups, chunk, basis), F32),
        in_specs=[pl.BlockSpec(memory_space=pltpu.VMEM)],
        out_specs=pl.BlockSpec(memory_space=pltpu.VMEM),
        scratch_shapes=[
            pltpu.VMEM((groups - 1, chunk, basis), F32),
            dma((groups - 1,)),
            dma((groups - 1,)),
            dma((blocks,)),
            dma((blocks,)),
            dma((blocks, groups // 2)),
            dma((blocks, groups // 2)),
            dma((blocks, groups // 2)),
            dma((blocks, groups // 2)),
        ],
        compiler_params=pltpu.CompilerParams(
            collective_id=0, has_side_effects=True, vmem_limit_bytes=32 * 1024 * 1024
        ),
    )(part)


def run_filter(rows, every):
    steps, _, basis = every.shape
    return pl.pallas_call(
        filter_kernel,
        out_shape=jax.ShapeDtypeStruct((steps, 8, basis), F32),
        in_specs=[pl.BlockSpec(memory_space=pltpu.VMEM)] * 2,
        out_specs=pl.BlockSpec(memory_space=pltpu.VMEM),
        scratch_shapes=[pltpu.VMEM((13, basis, basis), F32)],
        compiler_params=pltpu.CompilerParams(vmem_limit_bytes=32 * 1024 * 1024),
    )(rows, every)


def body(observed, slot_site, live_count, site_feature, site_precision, time_scale, variance):
    steps_local, slots_local = observed.shape
    basis = site_feature.shape[1]
    blocks, groups = lax.axis_size("tm"), lax.axis_size("obs")
    rank_of = jnp.arange(slots_local, dtype=jnp.int32)
    live = (rank_of[None, :] < live_count).astype(F32)
    table = site_precision.reshape(-1, 128)
    line = (slot_site[:, :, None] // 128 == jnp.arange(table.shape[0], dtype=jnp.int32)).astype(F32)
    lane = slot_site[:, :, None] % 128 == jnp.arange(128, dtype=jnp.int32)
    rows = jnp.einsum("tns,sl->tnl", line, table, precision=lax.Precision.HIGHEST)
    weight = jnp.sum(jnp.where(lane, rows, 0.0), axis=2) * live
    feature = site_feature[slot_site]
    weighted = feature * weight[:, :, None]
    values = jnp.broadcast_to(observed[:, :, None], (steps_local, slots_local, 16))
    sides = jnp.concatenate([feature, values], axis=2)
    part = jnp.einsum("tna,tnb->tab", sides, weighted, precision=lax.Precision.HIGHEST)
    height = basis + 16
    every = run_gather(part.reshape(groups, steps_local * height // groups, basis), blocks)
    every = every.reshape(blocks * steps_local, height, basis)
    means = run_filter(matern_rows(time_scale, variance), every)
    block = lax.axis_index("tm")
    return lax.dynamic_slice(means[:, 0, :], (block * steps_local, 0), (steps_local, basis))


def solution(mesh):
    in_specs = (P("tm", "obs"), P("tm", "obs"), P("tm", "obs"), P(), P(), P(), P())
    out_specs = P("tm", None)
    return jax.shard_map(body, mesh=mesh, in_specs=in_specs, out_specs=out_specs, check_vma=False)
```

```python
import functools

import jax
import jax.numpy as jnp
from jax import lax
from jax.experimental import pallas as pl
from jax.experimental.pallas import tpu as pltpu
from jax.sharding import PartitionSpec as P

F32 = jnp.float32
BF16 = jnp.bfloat16
MESH = pl.DeviceIdType.MESH


def dot_full(left, right):
    return jnp.dot(left, right, precision=lax.Precision.HIGHEST, preferred_element_type=F32)


def split(value):
    high = value.astype(BF16)
    return high, (value - high.astype(F32)).astype(BF16)


def dot_three(left, right):
    left_high, left_low = split(left)
    right_high, right_low = split(right)
    sides = jnp.concatenate([left_high, left_low], axis=1)
    tops = jnp.concatenate([right_high, right_high], axis=0)
    first = jnp.dot(sides, tops, preferred_element_type=F32)
    return first + jnp.dot(left_high, right_low, preferred_element_type=F32)


def matern_rows(time_scale, variance):
    rate = jnp.sqrt(F32(3.0)) / time_scale
    decay = jnp.exp(-rate)
    twice = 2.0 * rate
    decay_two = jnp.exp(-twice)
    term_now = twice**3 / 6.0
    series = term_now
    for degree in range(4, 17):
        term_now = term_now * twice / degree
        series = series + term_now
    noise_pp = variance * decay_two * series
    noise_pv = 2.0 * rate**3 * decay_two * variance
    noise_vv = rate**2 * variance * decay_two * (jnp.expm1(twice) + twice - 0.5 * twice**2)
    rows = [
        decay * (1.0 + rate),
        decay,
        -(rate**2) * decay,
        decay * (1.0 - rate),
        noise_pp,
        noise_pv,
        noise_vv,
        variance,
        rate**2 * variance,
    ]
    rows += [jnp.zeros_like(rate)] * (16 - len(rows))
    return jnp.stack(rows)


def filter_kernel(rows_ref, every_ref, mean_ref, coef_ref):
    steps, _, basis = every_ref.shape
    row_i = lax.broadcasted_iota(jnp.int32, (basis, basis), 0)
    col_i = lax.broadcasted_iota(jnp.int32, (basis, basis), 1)
    eye = (row_i == col_i).astype(F32)

    def wide(index):
        return jnp.broadcast_to(rows_ref[index : index + 1, :], (basis, basis))

    right = [wide(index) for index in range(4)]
    left = [value.T for value in right]
    pairs = [(0, 0), (0, 1), (1, 1), (0, 2), (1, 2), (0, 3), (1, 3), (2, 2), (2, 3), (3, 3)]
    for place, (one, two) in enumerate(pairs):
        scale = 0.5 if one == two else 1.0
        coef_ref[place] = scale * left[one] * right[two]
    coef_ref[10] = 0.5 * wide(4) * eye
    coef_ref[11] = wide(5) * eye
    coef_ref[12] = 0.5 * wide(6) * eye
    for place, (one, two) in enumerate(pairs[3:7]):
        coef_ref[13 + place] = left[two] * right[one]
    step_a = rows_ref[0:1, :]
    step_b = rows_ref[1:2, :]
    step_c = rows_ref[2:3, :]
    step_d = rows_ref[3:4, :]

    def advance(step, carry):
        cov_pp, cov_pv, cov_vp, cov_vv, mean_p, mean_v = carry
        gram = every_ref[step, :basis, :]
        info = every_ref[step, basis : basis + 8, :]
        both = jnp.concatenate([cov_pp, cov_pv], axis=1)
        seen = dot_three(jnp.concatenate([cov_pp, cov_vp], axis=0), gram)
        target = eye + seen[:basis]
        bound = jnp.max(jnp.sum(jnp.abs(target), axis=0))
        scale = 2.0 / (1.0 + bound)
        start = jnp.concatenate([eye - scale * target, scale * eye], axis=0)

        def squaring(state):
            radius, pair = state
            product = dot_three(pair, pair[:basis])
            pair = jnp.concatenate([product[:basis], pair[basis:] + product[basis:]], axis=0)
            return radius * radius, pair

        _, pair = lax.while_loop(lambda s: s[0] > 3e-3, squaring, ((bound - 1.0) * 0.5 * scale, start))

        def polish(state):
            count, _, inverse = state
            rest = eye - dot_three(target, inverse)
            size = jnp.max(jnp.abs(rest))
            return count + 1, size, inverse + dot_three(inverse, rest)

        _, _, gain = lax.while_loop(
            lambda s: jnp.logical_and(s[0] < 12, s[1] > 2e-3),
            polish,
            (jnp.int32(0), F32(1.0), pair[basis:]),
        )
        both = dot_three(gain, both)
        new_pp = both[:, :basis]
        new_pv = both[:, basis:]
        new_vv = cov_vv - dot_three(seen[basis:], new_pv)
        residual = info - dot_full(mean_p, gram)
        moved = dot_full(residual, both)
        mean_p = mean_p + moved[:, :basis]
        mean_v = mean_v + moved[:, basis:]
        mean_ref[step] = mean_p
        new_vp = new_pv.T
        half_pp = coef_ref[0] * new_pp + coef_ref[1] * new_pv + coef_ref[2] * new_vv + coef_ref[10]
        half_vv = coef_ref[7] * new_pp + coef_ref[8] * new_pv + coef_ref[9] * new_vv + coef_ref[12]
        next_pv = (
            coef_ref[3] * new_pp
            + coef_ref[4] * new_vp
            + coef_ref[5] * new_pv
            + coef_ref[6] * new_vv
            + coef_ref[11]
        )
        next_vp = (
            coef_ref[13] * new_pp
            + coef_ref[14] * new_pv
            + coef_ref[15] * new_vp
            + coef_ref[16] * new_vv
            + coef_ref[11]
        )
        return (
            half_pp + half_pp.T,
            next_pv,
            next_vp,
            half_vv + half_vv.T,
            step_a * mean_p + step_b * mean_v,
            step_c * mean_p + step_d * mean_v,
        )

    zero_row = jnp.zeros((8, basis), F32)
    zero_mat = jnp.zeros((basis, basis), F32)
    first = (wide(7) * eye, zero_mat, zero_mat, wide(8) * eye, zero_row, zero_row)
    lax.fori_loop(0, steps, advance, first)


def gather_kernel(part_ref, all_ref, recv_ref, rs_send, rs_recv, tm_send, tm_recv, ob_send, ob_recv, side_send, side_recv):
    blocks, groups, chunk, _ = all_ref.shape
    block = lax.axis_index("tm")
    group = lax.axis_index("obs")

    def to_block(distance):
        return {"tm": lax.rem(block + distance, blocks)}

    def to_group(distance):
        return {"obs": lax.rem(group + distance, groups)}

    barrier = pltpu.get_barrier_semaphore()
    for distance in range(1, groups):
        pl.semaphore_signal(barrier, inc=1, device_id=to_group(distance), device_id_type=MESH)

    def greet(distance, carry):
        pl.semaphore_signal(barrier, inc=1, device_id=to_block(distance), device_id_type=MESH)
        return carry

    lax.fori_loop(1, blocks, greet, 0)
    pl.semaphore_wait(barrier, groups + blocks - 2)

    def scatter(distance):
        peer = lax.rem(group + distance, groups)
        return pltpu.make_async_remote_copy(
            src_ref=part_ref.at[peer],
            dst_ref=recv_ref.at[distance - 1],
            send_sem=rs_send.at[distance - 1],
            recv_sem=rs_recv.at[distance - 1],
            device_id=to_group(distance),
            device_id_type=MESH,
        )

    for distance in range(1, groups):
        scatter(distance).start()
    total = part_ref[group]
    for distance in range(1, groups):
        scatter(distance).wait_recv()
        total = total + recv_ref[distance - 1]
    all_ref[block, group] = total

    def along(distance, source):
        return pltpu.make_async_remote_copy(
            src_ref=all_ref.at[source, group],
            dst_ref=all_ref.at[source, group],
            send_sem=tm_send.at[distance],
            recv_sem=tm_recv.at[distance],
            device_id=to_block(distance),
            device_id_type=MESH,
        )

    pairs = groups // 2
    sibling = group + 1 - 2 * lax.rem(group, 2)

    def owner_of(member, step):
        return lax.rem(member - 2 * step + groups, groups)

    def across(distance, source, step, owner):
        return pltpu.make_async_remote_copy(
            src_ref=all_ref.at[source, owner],
            dst_ref=all_ref.at[source, owner],
            send_sem=ob_send.at[distance, step],
            recv_sem=ob_recv.at[distance, step],
            device_id=to_group(2 * step),
            device_id_type=MESH,
        )

    def aside(distance, source, step, owner):
        return pltpu.make_async_remote_copy(
            src_ref=all_ref.at[source, owner],
            dst_ref=all_ref.at[source, owner],
            send_sem=side_send.at[distance, step],
            recv_sem=side_recv.at[distance, step],
            device_id={"obs": sibling},
            device_id_type=MESH,
        )

    def send_along(distance, carry):
        along(distance, block).start()
        return carry

    def origin(distance):
        return lax.rem(block - distance + blocks, blocks)

    def share(distance):
        source = origin(distance)
        for step in range(1, pairs):
            across(distance, source, step, group).start()
        aside(distance, source, 0, group).start()

    def forward(distance):
        source = origin(distance)
        for step in range(1, pairs):
            owner = owner_of(group, step)
            across(distance, source, step, owner).wait_recv()
            aside(distance, source, step, owner).start()

    lax.fori_loop(1, blocks, send_along, 0)
    share(0)

    def relay(distance, carry):
        along(distance, origin(distance)).wait_recv()
        share(distance)
        forward(distance - 1)
        return carry

    lax.fori_loop(1, blocks, relay, 0)
    forward(blocks - 1)

    def finish(distance, carry):
        source = origin(distance)
        for step in range(pairs):
            aside(distance, source, step, owner_of(sibling, step)).wait_recv()
            aside(distance, source, step, owner_of(group, step)).wait_send()
        for step in range(1, pairs):
            across(distance, source, step, group).wait_send()
        return carry

    lax.fori_loop(0, blocks, finish, 0)

    def sent(distance, carry):
        along(distance, block).wait_send()
        return carry

    lax.fori_loop(1, blocks, sent, 0)
    for distance in range(1, groups):
        scatter(distance).wait_send()


def run_gather(part, blocks):
    groups, chunk, basis = part.shape
    dma = pltpu.SemaphoreType.DMA
    return pl.pallas_call(
        gather_kernel,
        out_shape=jax.ShapeDtypeStruct((blocks, groups, chunk, basis), F32),
        in_specs=[pl.BlockSpec(memory_space=pltpu.VMEM)],
        out_specs=pl.BlockSpec(memory_space=pltpu.VMEM),
        scratch_shapes=[
            pltpu.VMEM((groups - 1, chunk, basis), F32),
            dma((groups - 1,)),
            dma((groups - 1,)),
            dma((blocks,)),
            dma((blocks,)),
            dma((blocks, groups // 2)),
            dma((blocks, groups // 2)),
            dma((blocks, groups // 2)),
            dma((blocks, groups // 2)),
        ],
        compiler_params=pltpu.CompilerParams(
            collective_id=0, has_side_effects=True, vmem_limit_bytes=32 * 1024 * 1024
        ),
    )(part)


def run_filter(rows, every):
    steps, _, basis = every.shape
    return pl.pallas_call(
        filter_kernel,
        out_shape=jax.ShapeDtypeStruct((steps, 8, basis), F32),
        in_specs=[pl.BlockSpec(memory_space=pltpu.VMEM)] * 2,
        out_specs=pl.BlockSpec(memory_space=pltpu.VMEM),
        scratch_shapes=[pltpu.VMEM((17, basis, basis), F32)],
        compiler_params=pltpu.CompilerParams(vmem_limit_bytes=32 * 1024 * 1024),
    )(rows, every)


def body(observed, slot_site, live_count, site_feature, site_precision, time_scale, variance):
    steps_local, slots_local = observed.shape
    basis = site_feature.shape[1]
    blocks, groups = lax.axis_size("tm"), lax.axis_size("obs")
    rank_of = jnp.arange(slots_local, dtype=jnp.int32)
    live = (rank_of[None, :] < live_count).astype(F32)
    table = site_precision.reshape(-1, 128)
    line = (slot_site[:, :, None] // 128 == jnp.arange(table.shape[0], dtype=jnp.int32)).astype(F32)
    lane = slot_site[:, :, None] % 128 == jnp.arange(128, dtype=jnp.int32)
    rows = jnp.einsum("tns,sl->tnl", line, table, precision=lax.Precision.HIGHEST)
    weight = jnp.sum(jnp.where(lane, rows, 0.0), axis=2) * live
    feature = site_feature[slot_site]
    weighted = feature * weight[:, :, None]
    values = jnp.broadcast_to(observed[:, :, None], (steps_local, slots_local, 16))
    sides = jnp.concatenate([feature, values], axis=2)
    part = jnp.einsum("tna,tnb->tab", sides, weighted, precision=lax.Precision.HIGHEST)
    height = basis + 16
    every = run_gather(part.reshape(groups, steps_local * height // groups, basis), blocks)
    every = every.reshape(blocks * steps_local, height, basis)
    means = run_filter(matern_rows(time_scale, variance), every)
    block = lax.axis_index("tm")
    return lax.dynamic_slice(means[:, 0, :], (block * steps_local, 0), (steps_local, basis))


def solution(mesh):
    in_specs = (P("tm", "obs"), P("tm", "obs"), P("tm", "obs"), P(), P(), P(), P())
    out_specs = P("tm", None)
    return jax.shard_map(body, mesh=mesh, in_specs=in_specs, out_specs=out_specs, check_vma=False)
```
